32 devices in a mesh: seq: 16 (over z, y, x), tp: 2 (over core).
Axes of the slice: x: 2, y: 2, z: 4, core: 2. Of those that a mesh axis runs over, the one named last changes fastest.
Arguments:
- hidden: bfloat16 [4096, 1024], P('seq'), may hold values from -6 to 6
- norm1_gain: float32 [1024], replicated, may hold values from 0.25 to 1.75
- w_query: bfloat16 [1024, 256], P(None, 'tp'), may hold values from -3 to 3
- w_key: bfloat16 [1024, 128], P(None, 'tp'), may hold values from -2 to 2
- w_value: bfloat16 [1024, 128], P(None, 'tp'), may hold values from -0.1875 to 0.1875
- w_out: bfloat16 [256, 1024], P('tp'), may hold values from -0.375 to 0.375
- norm2_gain: float32 [1024], replicated, may hold values from 0.25 to 1.75
- w_gate: bfloat16 [16, 1024, 512], P('seq'), may hold values from -0.1875 to 0.1875
- w_up: bfloat16 [16, 1024, 512], P('seq'), may hold values from -0.1875 to 0.1875
- w_down: bfloat16 [16, 512, 1024], P('seq'), may hold values from -0.25 to 0.25
- cache_in: bfloat16 [144, 256, 2, 128], P('seq', None, 'tp'), may hold values from -48 to 48
- cache_len: int32 [2], replicated, may hold values from 0 to 16384, as said below
- block_table: int32 [144], replicated, may hold values from 0 to 143, each once
- routes: int32 [4096, 8], P(('seq', 'tp')), may hold values from 0 to 15, all different within a row; in each aligned block of 128 rows (0 to 127, 128 to 255, ...) at most 96 rows name the same one
- gate_w: float32 [4096, 8], P(('seq', 'tp')), may hold values from 0.05 to 0.35
Outputs:
- hidden_out: bfloat16 [4096, 1024], P(('seq', 'tp'))
- cache_out: bfloat16 [144, 256, 2, 128], P('seq', None, 'tp')
The draws below stay inside these ranges and needn't reach their ends.
Inputs may be any that keep to these rules, and one draw needn't show every extreme that they name: `cache_len`: some request holds exactly 16384 entries. `block_table`: each pool block appears once; pool block b lies on index b // 9 of seq. `routes`: each row names 8 different experts; among the rows of one device (aligned blocks of 128 rows) no expert is named more than 96 times, a bound that some block reaches.
All inputs are finite; a program needn't handle non-finite values.
Results may differ from the reference program's by a relative error of at most 0.035.
The reference program's roundings to bfloat16 on the way count: a program that leaves them out, or rounds other values in their place, can miss the bound.
Values may be sent and summed in bfloat16 or wider, within the bound.
A program may use at most 128 MiB of HBM per device.

```python
import math
import jax
import jax.numpy as jnp
import numpy as np
from jax import lax

D = 1024
HD = 64
GROUP = 2
FFN = 512
TOP = 8
STRETCH = 2048
LMAX = 16384
BS = 256
KV_HEADS = 2
HEADS = 4
EXPERTS = 16
TOKENS = 4096
REQS = 2
MAXB = 72
POOL = 144
ROWS = 128
CAP = 96
N_SEQ = 16
N_TP = 2


def draw_w_query(key, part):
    sample = jnp.clip(jax.random.normal(key, (D, HEADS * HD), jnp.float32), -6.0, 6.0) * (2.5 / math.sqrt(D))
    sample = jnp.clip(sample, -3.0, 3.0)
    return sample.astype(jnp.bfloat16)


def draw_w_key(key, part):
    sample = jnp.clip(jax.random.normal(key, (D, KV_HEADS * HD), jnp.float32), -6.0, 6.0) * (1.0 / math.sqrt(D))
    sample = jnp.clip(sample, -2.0, 2.0)
    return sample.astype(jnp.bfloat16)


def draw_cache_in(key, part):
    key_part = jax.random.fold_in(key, 11)
    value_part = jax.random.fold_in(key, 12)
    key_rows = jnp.clip(jax.random.normal(key_part, (POOL, BS, KV_HEADS, HD), jnp.float32), -6.0, 6.0)
    value_rows = jnp.clip(jax.random.normal(value_part, (POOL, BS, KV_HEADS, HD), jnp.float32), -6.0, 6.0)
    return jnp.concatenate([key_rows, value_rows], axis=-1).astype(jnp.bfloat16)


def draw_cache_len(key, part):
    length_part = jax.random.fold_in(key, 21)
    pick_part = jax.random.fold_in(key, 22)
    lengths = jax.random.randint(length_part, (REQS,), 0, LMAX + 1, jnp.int32)
    longest = jax.random.randint(pick_part, (), 0, REQS, jnp.int32)
    return jnp.where(jnp.arange(REQS, dtype=jnp.int32) == longest, LMAX, lengths).astype(jnp.int32)


def block_scale(own_key, extent, pieces, smallest, largest):
    def one(position, shards_of):
        draws = jax.random.uniform(jax.random.fold_in(jax.random.fold_in(own_key, 6), position), (shards_of,), jnp.float32, smallest / len(pieces), largest / len(pieces))
        return jnp.repeat(jnp.exp(draws), extent[position] // shards_of).reshape((-1,) + (1,) * (len(extent) - position - 1))

    loudness = one(*pieces[0])
    for cut in pieces[1:]:
        loudness = loudness * one(*cut)
    return loudness


def shared_out(stream_key, own, number, rows, amount, top, limit, lean):
    ranking = jax.random.permutation(stream_key, amount)
    packed, usual = load_shares(amount, rows * top, limit, lean, True), load_shares(amount, rows * top, limit, lean, False)
    places = jnp.arange(amount)

    def named(sizes, offset_by):
        used = int((sizes > 0).sum())
        fixed = max(1, used // 4)
        moved = fixed + (places - fixed + offset_by * (used - fixed)) % max(1, amount - fixed)
        return jnp.zeros((amount,), jnp.int32).at[ranking[jnp.where(places < fixed, places, moved)]].set(jnp.asarray(sizes, jnp.int32))

    sizes = jnp.where(number % 4 == 0, named(packed, number // 4), named(usual, number - number // 4 - 1))
    mixed = jax.random.permutation(jax.random.fold_in(own, 3), amount)
    donor, sink = mixed[0:amount // 2 * 2:2], mixed[1:amount // 2 * 2:2]
    room = jnp.minimum(sizes[donor] - 1, limit - sizes[sink]) // 2
    room = jnp.where((donor == ranking[0]) | (sink == ranking[0]) | (sizes[sink] == 0), 0, jnp.maximum(room, 0))
    moved = jax.random.randint(jax.random.fold_in(own, 4), (amount // 2,), 0, 1 << 20) % (room + 1)
    sizes = sizes.at[donor].add(-moved).at[sink].add(moved)
    labels = jnp.searchsorted(jnp.cumsum(sizes), jnp.arange(rows * top), side="right").astype(jnp.int32)
    grid = labels.reshape(top, rows).T
    grid = grid[jax.random.permutation(jax.random.fold_in(own, 1), rows)]
    offset_by = jax.random.randint(jax.random.fold_in(own, 2), (rows, 1), 0, top)
    return jnp.take_along_axis(grid, (jnp.arange(top)[None, :] + offset_by) % top, axis=1)


def load_shares(amount, total, bound, lean, full):
    weights = [(1 << 20) // math.isqrt(standing ** lean) + 1 for standing in range(1, amount + 1)]
    largest = bound if full else min(bound, max(-(-total // amount), total * weights[0] // sum(weights)))
    least = 1 if total - largest >= amount - 1 else 0
    given, spare = [largest] + [least] * (amount - 1), total - largest - least * (amount - 1)
    while spare > 0:
        movable = [i for i in range(1, amount) if given[i] < largest] or [i for i in range(1, amount) if given[i] < bound]
        pool, budget = sum([weights[i] for i in movable]), spare
        for i in movable:
            more = min(bound - given[i], max(1, budget * weights[i] // pool), spare)
            given[i] = given[i] + more
            spare = spare - more
    return np.array(given)


def scatter_about(stream_key, extent, width, limit, pieces=(), held_as=jnp.bfloat16):
    array = width * jax.random.normal(stream_key, extent, jnp.float32)
    if pieces:
        array = array * block_scale(stream_key, extent, pieces, -0.22, 0.18)
    return jnp.clip(array, -limit, limit).astype(held_as)


def setup_inputs(seed: int = 0) -> dict:
    arg_keys = jax.random.split(jax.random.key(seed), 16)
    hidden = scatter_about(arg_keys[0], (TOKENS, D), 1.0, 6.0, ((0, 16),))
    norm1_gain = jnp.clip(1.0 + 0.15 * jax.random.normal(arg_keys[1], (D,), jnp.float32), 0.25, 1.75)
    w_query = draw_w_query(jax.random.fold_in(arg_keys[15], 71), 0)
    w_key = draw_w_key(jax.random.fold_in(arg_keys[15], 71), 0)
    w_value = scatter_about(arg_keys[4], (D, KV_HEADS * HD), D ** -0.5, 0.1875, ((1, 2),))
    w_out = scatter_about(arg_keys[5], (HEADS * HD, D), (HEADS * HD) ** -0.5, 0.375, ((0, 2),))
    norm2_gain = jnp.clip(1.0 + 0.15 * jax.random.normal(arg_keys[6], (D,), jnp.float32), 0.25, 1.75)
    w_gate = scatter_about(arg_keys[7], (EXPERTS, D, FFN), D ** -0.5, 0.1875, ((0, 16),))
    w_up = scatter_about(arg_keys[8], (EXPERTS, D, FFN), D ** -0.5, 0.1875, ((0, 16),))
    w_down = scatter_about(arg_keys[9], (EXPERTS, FFN, D), FFN ** -0.5, 0.25, ((0, 16),))
    cache_in = draw_cache_in(jax.random.fold_in(arg_keys[15], 71), 0)
    cache_len = draw_cache_len(jax.random.fold_in(arg_keys[15], 71), 0)
    block_table = jax.random.permutation(arg_keys[12], POOL).astype(jnp.int32)
    routes_keys = jax.random.split(jax.random.fold_in(arg_keys[13], 1), TOKENS // ROWS)
    routes_turns = jax.random.permutation(jax.random.fold_in(arg_keys[13], 3), TOKENS // ROWS)
    routes = jax.vmap(lambda own, number: shared_out(jax.random.fold_in(arg_keys[13], 2), own, number, ROWS, EXPERTS, TOP, CAP, 2))(routes_keys, routes_turns).reshape((TOKENS, TOP))
    gate_w = jnp.clip(0.05 + 0.29999999 * jax.random.uniform(arg_keys[14], (TOKENS, TOP), jnp.float32) ** block_scale(arg_keys[14], (TOKENS, TOP), ((0, 32),), -0.2, 0.2), 0.05, 0.35)
    return dict(hidden=hidden, norm1_gain=norm1_gain, w_query=w_query, w_key=w_key, w_value=w_value, w_out=w_out, norm2_gain=norm2_gain, w_gate=w_gate, w_up=w_up, w_down=w_down, cache_in=cache_in, cache_len=cache_len, block_table=block_table, routes=routes, gate_w=gate_w)


norm_eps = 1e-05
rope_base = 10000.0
mask_fill = -1e+30

def rms_scale(inputs, gains):
    floats = inputs.astype(jnp.float32)
    mean_square = lax.optimization_barrier(jnp.mean(floats * floats, axis=-1, keepdims=True))
    return (floats * lax.rsqrt(mean_square + norm_eps) * gains).astype(jnp.bfloat16)

def rotate(vectors, positions):
    halfway = vectors.shape[-1] // 2
    counter = jnp.arange(halfway, dtype=jnp.int32).astype(jnp.float32)
    frequency = jnp.exp(counter * (-2.0 * math.log(rope_base) / vectors.shape[-1]))
    angles = positions.astype(jnp.float32)[:, None] * frequency[None, :]
    cosine = jnp.cos(angles)[:, None, :]
    sine_part = jnp.sin(angles)[:, None, :]
    front_half = vectors[..., :halfway]
    back_half = vectors[..., halfway:]
    return jnp.concatenate([front_half * cosine - back_half * sine_part, back_half * cosine + front_half * sine_part], axis=-1)

def attend(operands):
    queries, page, fresh_keys, fresh_values, filled = operands
    span = page.shape[0]
    head_dim = fresh_keys.shape[-1]
    fresh_len = fresh_keys.shape[0]
    all_keys = jnp.concatenate([page[:, :head_dim], fresh_keys], axis=0).astype(jnp.float32)
    all_values = jnp.concatenate([page[:, head_dim:], fresh_values], axis=0).astype(jnp.float32)
    scores = jnp.einsum('chd,kd->chk', queries.astype(jnp.float32), all_keys) * (1.0 / math.sqrt(head_dim))
    old_live = jnp.arange(span, dtype=jnp.int32) < filled
    causal = jnp.arange(fresh_len, dtype=jnp.int32)[None, :] <= jnp.arange(fresh_len, dtype=jnp.int32)[:, None]
    allowed = jnp.concatenate([jnp.broadcast_to(old_live[None, :], (fresh_len, span)), causal], axis=1)[:, None, :]
    scores = jnp.where(allowed, scores, mask_fill)
    peak = lax.optimization_barrier(jnp.max(scores, axis=-1, keepdims=True))
    weights = jnp.where(allowed, jnp.exp(scores - peak), 0.0)
    denom = lax.optimization_barrier(jnp.sum(weights, axis=-1))
    rounded = lax.optimization_barrier(weights.astype(jnp.bfloat16)).astype(jnp.float32)
    mixed = jnp.einsum('chk,kd->chd', rounded, all_values)
    return mixed / denom[..., None]

def take_rows(table_rows, picks):
    return table_rows[picks]

def reference(hidden, norm1_gain, w_query, w_key, w_value, w_out, norm2_gain, w_gate, w_up, w_down, cache_in, cache_len, block_table, routes, gate_w):
    token_ids = jnp.arange(TOKENS, dtype=jnp.int32)
    positions = cache_len[token_ids // STRETCH] + token_ids % STRETCH
    normed = rms_scale(hidden, norm1_gain)
    queries = jnp.dot(normed, w_query, preferred_element_type=jnp.float32).reshape(TOKENS, HEADS, HD)
    queries = rotate(queries, positions).astype(jnp.bfloat16)
    key_rows = jnp.dot(normed, w_key, preferred_element_type=jnp.float32).reshape(TOKENS, KV_HEADS, HD)
    key_rows = rotate(key_rows, positions).astype(jnp.bfloat16)
    value_rows = jnp.dot(normed, w_value, preferred_element_type=jnp.float32).reshape(TOKENS, KV_HEADS, HD).astype(jnp.bfloat16)
    span = MAXB * BS
    pages = cache_in[block_table.reshape(REQS, MAXB)].reshape(REQS, span, KV_HEADS, 2 * HD)
    per_query = queries.reshape(REQS, STRETCH, KV_HEADS, GROUP, HD).transpose(0, 2, 1, 3, 4).reshape(REQS * KV_HEADS, STRETCH, GROUP, HD)
    per_page = pages.transpose(0, 2, 1, 3).reshape(REQS * KV_HEADS, span, 2 * HD)
    per_key = key_rows.reshape(REQS, STRETCH, KV_HEADS, HD).transpose(0, 2, 1, 3).reshape(REQS * KV_HEADS, STRETCH, HD)
    per_value = value_rows.reshape(REQS, STRETCH, KV_HEADS, HD).transpose(0, 2, 1, 3).reshape(REQS * KV_HEADS, STRETCH, HD)
    per_fill = jnp.repeat(cache_len, KV_HEADS)
    mixed = lax.map(attend, (per_query, per_page, per_key, per_value, per_fill))
    attention = mixed.reshape(REQS, KV_HEADS, STRETCH, GROUP, HD).transpose(0, 2, 1, 3, 4).reshape(TOKENS, HEADS * HD).astype(jnp.bfloat16)
    residual = (hidden.astype(jnp.float32) + jnp.dot(attention, w_out, preferred_element_type=jnp.float32)).astype(jnp.bfloat16)
    normed2 = rms_scale(residual, norm2_gain)
    bound_rows = N_SEQ * N_TP * CAP

    def one_expert(totals, expert_id):
        matches = routes == expert_id
        chosen = jnp.any(matches, axis=1)
        weights = lax.optimization_barrier(jnp.sum(jnp.where(matches, gate_w, 0.0), axis=1))
        picks = jnp.nonzero(chosen, size=bound_rows, fill_value=0)[0].astype(jnp.int32)
        usable = jnp.arange(bound_rows, dtype=jnp.int32) < jnp.sum(chosen.astype(jnp.int32))
        inputs = normed2[picks]
        gate_part = jnp.dot(inputs, w_gate[expert_id], preferred_element_type=jnp.float32)
        up_part = jnp.dot(inputs, w_up[expert_id], preferred_element_type=jnp.float32)
        inner = (jax.nn.silu(gate_part) * up_part).astype(jnp.bfloat16)
        output = jnp.dot(inner, w_down[expert_id], preferred_element_type=jnp.float32).astype(jnp.bfloat16)
        term = jnp.where(usable[:, None], weights[picks][:, None] * output.astype(jnp.float32), 0.0)
        return (totals.at[picks].add(term), None)
    moe_total, unused = lax.scan(one_expert, jnp.zeros((TOKENS, D), jnp.float32), jnp.arange(EXPERTS, dtype=jnp.int32))
    hidden_out = (residual.astype(jnp.float32) + moe_total).astype(jnp.bfloat16)
    fresh_rows = jnp.concatenate([key_rows, value_rows], axis=-1).reshape(REQS, STRETCH, KV_HEADS, 2 * HD)
    place = jnp.arange(span, dtype=jnp.int32)[None, :]
    filled = cache_len[:, None]
    inside = (place >= filled) & (place < filled + STRETCH)
    source = jnp.clip(place - filled, 0, STRETCH - 1).astype(jnp.int32)
    fresh = jax.vmap(take_rows)(fresh_rows, source)
    merged = jnp.where(inside[:, :, None, None], fresh, pages).reshape(POOL, BS, KV_HEADS, 2 * HD)
    cache_out = jnp.zeros_like(cache_in).at[block_table].set(merged)
    return (hidden_out, cache_out)
```

```python
import functools
import math

import jax
import jax.numpy as jnp
from jax import lax
from jax.experimental import pallas as pl
from jax.experimental.pallas import tpu as pltpu
from jax.sharding import PartitionSpec as P

D = 1024
HD = 64
GROUP = 2
STRETCH = 2048
BS = 256
TOK_DEV = 256
MAXB = 72
SPAN = STRETCH // TOK_DEV

norm_eps = 1e-05
rope_base = 10000.0
mask_fill = -1e30
MESH = pl.DeviceIdType.MESH
F32 = jnp.float32
BF16 = jnp.bfloat16


def bit_orders(bits, count):
    low = list(range(bits - 1))
    orders = []
    for part in range(count):
        turn = part % max(1, len(low))
        orders.append([bits - 1] + low[turn:] + low[:turn])
    return orders


def flip(place, rel, bits):
    out = place
    for bit in range(bits):
        if rel >> bit & 1:
            out = out + (1 - 2 * (place // (1 << bit) % 2)) * (1 << bit)
    return out


def slot_in(order, place, other):
    out = 0
    for step, bit in enumerate(order):
        out = out + (place // (1 << bit) + other // (1 << bit)) % 2 * (1 << step)
    return out


def rel_of(order, slot):
    return sum(1 << bit for step, bit in enumerate(order) if slot >> step & 1)


def row_parts(rows):
    units = rows // 16
    count = min(3, units)
    sizes = [(units // count + (1 if i < units % count else 0)) * 16 for i in range(count)]
    return [(sum(sizes[:i]), size) for i, size in enumerate(sizes)]


def scaled(floats, gains):
    mean_square = jnp.mean(floats * floats, axis=-1, keepdims=True)
    return (floats * lax.rsqrt(mean_square + norm_eps) * gains).astype(BF16)


def project_kernel(bits, hidden, gain, wq, wkv, cosine, sine, buf, send, recv):
    me, tp = lax.axis_index("seq"), lax.axis_index("tp")
    barrier = pltpu.get_barrier_semaphore()
    for bit in range(bits):
        pl.semaphore_signal(
            barrier, inc=1, device_id=(flip(me, 1 << bit, bits), tp), device_id_type=MESH
        )
    normed = scaled(hidden[...].astype(F32), gain[...])
    cos, sin = cosine[...], sine[...]

    def turned(rows):
        a, b = rows[:32], rows[32:]
        return jnp.concatenate([a * cos - b * sin, b * cos + a * sin], axis=0)

    q = jnp.dot(normed, wq[...], preferred_element_type=F32).T
    kv = jnp.dot(normed, wkv[...], preferred_element_type=F32).T
    buf[0, 0] = (turned(q[:HD]) * 0.125).astype(BF16)
    buf[1, 0] = (turned(q[HD:]) * 0.125).astype(BF16)
    buf[2, 0] = turned(kv[:HD]).astype(BF16)
    buf[3, 0] = kv[HD:].astype(BF16)
    pl.semaphore_wait(barrier, bits)
    orders = bit_orders(bits, 4)
    copies = {}
    for step in range(bits):
        size = 1 << step
        for part in range(4):
            if step:
                copies[part, step - 1].wait_recv()
            copy = pltpu.make_async_remote_copy(
                src_ref=buf.at[part, pl.ds(0, size)],
                dst_ref=buf.at[part, pl.ds(size, size)],
                send_sem=send.at[part, step],
                recv_sem=recv.at[part, step],
                device_id=(flip(me, 1 << orders[part][step], bits), tp),
                device_id_type=MESH,
            )
            copy.start()
            copies[part, step] = copy
    for part in range(4):
        copies[part, bits - 1].wait_recv()
    for copy in copies.values():
        copy.wait_send()


CHUNK = 4


def cache_kernel(
    bits, slots, lens, buf, cache, gates, acc_out, stat_out, cache_out, vt, peak, mass, accum
):
    me = lax.axis_index("seq")
    seq_count = 1 << bits
    blocks = cache.shape[0]
    orders = bit_orders(bits, 4)

    def place_block(b, carry):
        slot = slots[b]
        request = slot // MAXB
        shift = slot % MAXB * BS - lens[request]
        vt[b] = cache[b][:, HD:].astype(F32).T.astype(BF16)
        cache_out[b] = cache[b]

        @pl.when((shift > -BS) & (shift < STRETCH))
        def _():
            first = (shift + STRETCH) // TOK_DEV - SPAN
            entry = lax.broadcasted_iota(jnp.int32, (BS, TOK_DEV), 0)
            token = lax.broadcasted_iota(jnp.int32, (BS, TOK_DEV), 1)
            keys = jnp.zeros((BS, HD), F32)
            values = jnp.zeros((BS, HD), F32)
            for extra in range(2):
                window = first + extra
                held = request * SPAN + jnp.clip(window, 0, SPAN - 1)
                hit = (entry + (shift - window * TOK_DEV) == token) & (window >= 0) & (
                    window < SPAN
                )
                pick = jnp.where(hit, 1.0, 0.0).astype(BF16)
                dims = (((1,), (1,)), ((), ()))
                keys += lax.dot_general(
                    pick, buf[2, slot_in(orders[2], me, held)], dims, preferred_element_type=F32
                )
                values += lax.dot_general(
                    pick, buf[3, slot_in(orders[3], me, held)], dims, preferred_element_type=F32
                )
            row = lax.broadcasted_iota(jnp.int32, (BS, 2 * HD), 0) + shift
            fresh = jnp.concatenate([keys, values], axis=1)
            inside = (row >= 0) & (row < STRETCH)
            cache_out[b] = jnp.where(inside, fresh, cache[b].astype(F32)).astype(BF16)

        return carry

    lax.fori_loop(0, blocks, place_block, 0)

    def group(g, carry):
        request = g * CHUNK // SPAN
        filled = lens[request]
        peak[...] = jnp.full_like(peak, mask_fill)
        mass[...] = jnp.zeros_like(mass)
        accum[...] = jnp.zeros_like(accum)

        def visit(b, inner):
            slot = slots[b]
            first = slot % MAXB * BS

            @pl.when((slot // MAXB == request) & (first < filled))
            def _():
                keys = cache[b][:, :HD]
                values = vt[b]
                row = lax.broadcasted_iota(jnp.int32, (BS, GROUP * TOK_DEV), 0)
                seen = row < filled - first
                for c in range(CHUNK):
                    s = g * CHUNK + c
                    query = jnp.concatenate(
                        [buf[0, slot_in(orders[0], me, s)], buf[1, slot_in(orders[1], me, s)]],
                        axis=1,
                    )
                    scores = jnp.dot(keys, query, preferred_element_type=F32)
                    scores = jnp.where(seen, scores, mask_fill)
                    old = peak[c]
                    new = jnp.maximum(old, jnp.max(scores, axis=0, keepdims=True))
                    weights = jnp.exp(scores - new)
                    retain = jnp.exp(old - new)
                    peak[c] = new
                    mass[c] = mass[c] * retain + jnp.sum(weights, axis=0, keepdims=True)
                    accum[c] = accum[c] * retain + jnp.dot(
                        values, weights.astype(BF16), preferred_element_type=F32
                    )

            return inner

        lax.fori_loop(0, blocks, visit, 0)
        for c in range(CHUNK):
            s = g * CHUNK + c
            a = accum[c]
            acc_out[s] = jnp.concatenate([a[:, :TOK_DEV], a[:, TOK_DEV:]], axis=0).astype(BF16)
            m, l = peak[c], mass[c]
            stat_out[s] = jnp.concatenate(
                [
                    m[:, :TOK_DEV],
                    m[:, TOK_DEV:],
                    l[:, :TOK_DEV],
                    l[:, TOK_DEV:],
                    gates[s],
                    jnp.zeros((3, TOK_DEV), F32),
                ],
                axis=0,
            )
        return carry

    lax.fori_loop(0, seq_count // CHUNK, group, 0)


def tail_kernel(
    bits,
    tp_count,
    acc,
    stat,
    buf,
    own_hidden,
    w_out,
    gain,
    w_gate,
    w_up,
    w_down,
    out,
    racc,
    rstat,
    full,
    part_out,
    part_in,
    residual,
    *rest,
):
    me, tp = lax.axis_index("seq"), lax.axis_index("tp")
    seq_count = 1 << bits
    rows = own_hidden.shape[0]
    parts = row_parts(rows)
    count = len(parts)
    xs, ys, zs = rest[:count], rest[count : 2 * count], rest[2 * count : 3 * count]
    acc_send, acc_recv, st_send, st_recv, tp_send, tp_recv, ag_send, ag_recv, rs_send, rs_recv = (
        rest[3 * count :]
    )
    barrier = pltpu.get_barrier_semaphore()
    for rel in range(1, seq_count):
        pl.semaphore_signal(
            barrier, inc=1, device_id=(flip(me, rel, bits), tp), device_id_type=MESH
        )
    for turn in range(1, tp_count):
        pl.semaphore_signal(
            barrier, inc=1, device_id=(me, (tp + turn) % tp_count), device_id_type=MESH
        )
    pl.semaphore_wait(barrier, seq_count - 1 + tp_count - 1)
    copies = []
    for rel in range(seq_count - 1, 0, -1):
        dest = flip(me, rel, bits)
        for src, dst, send, recv in (
            (stat, rstat, st_send, st_recv),
            (acc, racc, acc_send, acc_recv),
        ):
            copy = pltpu.make_async_remote_copy(
                src_ref=src.at[dest],
                dst_ref=dst.at[rel],
                send_sem=send.at[rel],
                recv_sem=recv.at[rel],
                device_id=(dest, tp),
                device_id_type=MESH,
            )
            copy.start()
            copies.append(copy)
    racc[0] = acc[me]
    rstat[0] = stat[me]
    orders = bit_orders(bits, 4)
    local = me % SPAN
    base = me - local
    query = jnp.concatenate([buf[0, 0], buf[1, 0]], axis=1)
    width = GROUP * TOK_DEV
    key_row = lax.broadcasted_iota(jnp.int32, (TOK_DEV, width), 0)
    query_col = lax.broadcasted_iota(jnp.int32, (TOK_DEV, width), 1) % TOK_DEV

    def own(j, states):
        old, mass, accum = states
        keys = buf[2, slot_in(orders[2], me, base + j)]
        values = buf[3, slot_in(orders[3], me, base + j)]
        scores = lax.dot_general(
            keys, query, (((0,), (0,)), ((), ())), preferred_element_type=F32
        )
        scores = jnp.where(key_row + (j - local) * TOK_DEV <= query_col, scores, mask_fill)
        new = jnp.maximum(old, jnp.max(scores, axis=0, keepdims=True))
        weights = jnp.exp(scores - new)
        retain = jnp.exp(old - new)
        mass = mass * retain + jnp.sum(weights, axis=0, keepdims=True)
        accum = accum * retain + jnp.dot(
            values, weights.astype(BF16), preferred_element_type=F32
        )
        return new, mass, accum

    self_peak, self_mass, self_accum = lax.fori_loop(
        0,
        local + 1,
        own,
        (
            jnp.full((1, width), mask_fill, F32),
            jnp.zeros((1, width), F32),
            jnp.zeros((HD, width), F32),
        ),
    )
    for copy in copies:
        copy.wait_recv()
    heads = []
    for head in range(GROUP):
        lanes = slice(head * TOK_DEV, (head + 1) * TOK_DEV)
        top = self_peak[:, lanes]
        for rel in range(seq_count):
            top = jnp.maximum(top, rstat[rel, head : head + 1, :])
        share = jnp.exp(self_peak[:, lanes] - top)
        denom = self_mass[:, lanes] * share
        total = self_accum[:, lanes] * share
        for rel in range(seq_count):
            share = jnp.exp(rstat[rel, head : head + 1, :] - top)
            denom += rstat[rel, GROUP + head : GROUP + head + 1, :] * share
            total += racc[rel, head * HD : (head + 1) * HD, :].astype(F32) * share
        heads.append(total / denom)
    attention = jnp.concatenate(heads, axis=0).T.astype(BF16)
    product = jnp.dot(attention, w_out[...], preferred_element_type=F32)
    for turn in range(tp_count):
        piece = product[turn * rows : (turn + 1) * rows]
        full[turn] = piece
        part_out[turn] = piece.astype(BF16)
    swaps = []
    for turn in range(1, tp_count):
        peer = (tp + turn) % tp_count
        copy = pltpu.make_async_remote_copy(
            src_ref=part_out.at[peer],
            dst_ref=part_in.at[turn - 1],
            send_sem=tp_send.at[turn - 1],
            recv_sem=tp_recv.at[turn - 1],
            device_id=(me, peer),
            device_id_type=MESH,
        )
        copy.start()
        swaps.append(copy)
    gate_cols = rstat[:, :, :128].reshape(seq_count * 8, 128).T
    head_total = full[tp]
    for turn in range(1, tp_count):
        swaps[turn - 1].wait_recv()
        head_total += part_in[turn - 1].astype(F32)
    rounded = (own_hidden[...].astype(F32) + head_total).astype(BF16)
    residual[...] = rounded
    normed = scaled(rounded.astype(F32), gain[...])
    for part, (start, size) in enumerate(parts):
        xs[part][pl.ds(0, size), :] = normed[start : start + size]
    walks = bit_orders(bits, count)

    def experts(part, low, high):
        start, size = parts[part]
        span = pl.ds(low * size, (high - low) * size)
        x = xs[part][span, :]
        gate_part = jnp.dot(x, w_gate[...], preferred_element_type=F32)
        up_part = jnp.dot(x, w_up[...], preferred_element_type=F32)
        inner = (gate_part / (1.0 + jnp.exp(-gate_part)) * up_part).astype(BF16)
        answer = jnp.dot(inner, w_down[...], preferred_element_type=F32).astype(BF16)
        weight = jnp.concatenate(
            [
                gate_cols[start : start + size, col : col + 1]
                for col in (8 * rel_of(walks[part], slot) + 4 for slot in range(low, high))
            ],
            axis=0,
        )
        ys[part][span, :] = (answer.astype(F32) * weight).astype(BF16)

    gathers, sums = {}, {}
    for step in range(bits):
        for part, (start, size) in enumerate(parts):
            if step:
                gathers[part, step - 1].wait_recv()
            extent = size << step
            copy = pltpu.make_async_remote_copy(
                src_ref=xs[part].at[pl.ds(0, extent), :],
                dst_ref=xs[part].at[pl.ds(extent, extent), :],
                send_sem=ag_send.at[part, step],
                recv_sem=ag_recv.at[part, step],
                device_id=(flip(me, 1 << walks[part][step], bits), tp),
                device_id_type=MESH,
            )
            copy.start()
            gathers[part, step] = copy
        if step >= 2:
            for part in range(count):
                experts(part, 0 if step == 2 else 1 << (step - 1), 1 << step)

    def send_sum(part, step):
        extent = parts[part][1] << step
        copy = pltpu.make_async_remote_copy(
            src_ref=ys[part].at[pl.ds(extent, extent), :],
            dst_ref=zs[part].at[pl.ds(extent, extent), :],
            send_sem=rs_send.at[part, step],
            recv_sem=rs_recv.at[part, step],
            device_id=(flip(me, 1 << walks[part][step], bits), tp),
            device_id_type=MESH,
        )
        copy.start()
        sums[part, step] = copy

    for part in range(count):
        gathers[part, bits - 1].wait_recv()
        experts(part, seq_count // 2, seq_count)
        send_sum(part, bits - 1)

    def arrived(part, step, low, high):
        extent = parts[part][1] << step
        mine = ys[part][pl.ds(low, high - low), :].astype(F32)
        return mine + zs[part][pl.ds(extent + low, high - low), :].astype(F32)

    for step in range(bits - 1, 0, -1):
        for part, (start, size) in enumerate(parts):
            extent = size << step
            half = extent // 2
            sums[part, step].wait_recv()
            ys[part][pl.ds(half, half), :] = arrived(part, step, half, extent).astype(BF16)
            send_sum(part, step - 1)
        for part, (start, size) in enumerate(parts):
            half = (size << step) // 2
            ys[part][pl.ds(0, half), :] = arrived(part, step, 0, half).astype(BF16)
    for part, (start, size) in enumerate(parts):
        sums[part, 0].wait_recv()
        total = arrived(part, 0, 0, size)
        out[pl.ds(start, size), :] = (
            residual[pl.ds(start, size), :].astype(F32) + total
        ).astype(BF16)
    for copy in copies + swaps + list(gathers.values()) + list(sums.values()):
        copy.wait_send()


def on_device(
    hidden,
    norm1_gain,
    w_query,
    w_key,
    w_value,
    w_out,
    norm2_gain,
    w_gate,
    w_up,
    w_down,
    cache_in,
    cache_len,
    block_table,
    routes,
    gate_w,
):
    seq_count = lax.axis_size("seq")
    tp_count = lax.axis_size("tp")
    bits = seq_count.bit_length() - 1
    seq_place = lax.axis_index("seq")
    tp_place = lax.axis_index("tp")
    vmem = pl.BlockSpec(memory_space=pltpu.VMEM)
    smem = pl.BlockSpec(memory_space=pltpu.SMEM)
    request = seq_place * TOK_DEV // STRETCH
    token = seq_place * TOK_DEV % STRETCH + jnp.arange(TOK_DEV, dtype=jnp.int32)
    positions = cache_len[request] + token
    counter = jnp.arange(HD // 2, dtype=jnp.int32).astype(F32)
    frequency = jnp.exp(counter * (-2.0 * math.log(rope_base) / HD))
    angles = positions.astype(F32)[None, :] * frequency[:, None]
    w_kv = jnp.concatenate([w_key, w_value], axis=1)
    dma = pltpu.SemaphoreType.DMA
    buf = pl.pallas_call(
        functools.partial(project_kernel, bits),
        out_shape=jax.ShapeDtypeStruct((4, seq_count, HD, TOK_DEV), BF16),
        in_specs=[vmem] * 6,
        out_specs=vmem,
        scratch_shapes=[dma((4, bits)), dma((4, bits))],
        compiler_params=pltpu.CompilerParams(
            collective_id=0, has_side_effects=True, vmem_limit_bytes=32 << 20
        ),
        name="project",
    )(hidden, norm1_gain[None, :], w_query, w_kv, jnp.cos(angles), jnp.sin(angles))

    blocks = cache_in.shape[0]
    pool_ids = seq_place * blocks + jnp.arange(blocks, dtype=jnp.int32)
    places = jnp.arange(block_table.shape[0], dtype=jnp.int32)
    slots = jnp.sum(
        jnp.where(block_table[None, :] == pool_ids[:, None], places[None, :], 0), axis=1
    )
    rows = TOK_DEV // tp_count
    experts = jnp.arange(seq_count, dtype=jnp.int32)
    gates = jnp.sum(
        jnp.where(routes.T[None] == experts[:, None, None], gate_w.T[None], 0.0), axis=1
    )
    gates = jnp.pad(gates, ((0, 0), (0, TOK_DEV - rows)))[:, None, :]
    width = GROUP * TOK_DEV
    acc, stat, cache_out = pl.pallas_call(
        functools.partial(cache_kernel, bits),
        out_shape=(
            jax.ShapeDtypeStruct((seq_count, GROUP * HD, TOK_DEV), BF16),
            jax.ShapeDtypeStruct((seq_count, 8, TOK_DEV), F32),
            jax.ShapeDtypeStruct((blocks, BS, 2 * HD), BF16),
        ),
        in_specs=[smem, smem, vmem, vmem, vmem],
        out_specs=(vmem, vmem, vmem),
        scratch_shapes=[
            pltpu.VMEM((blocks, HD, BS), BF16),
            pltpu.VMEM((CHUNK, 1, width), F32),
            pltpu.VMEM((CHUNK, 1, width), F32),
            pltpu.VMEM((CHUNK, HD, width), F32),
        ],
        compiler_params=pltpu.CompilerParams(vmem_limit_bytes=40 << 20),
        name="cached",
    )(slots, cache_len, buf, cache_in.reshape(blocks, BS, 2 * HD), gates)

    own_hidden = lax.dynamic_slice_in_dim(hidden, tp_place * rows, rows, 0)
    parts = row_parts(rows)
    held = [pltpu.VMEM((seq_count * size, D), BF16) for _, size in parts]
    count = len(parts)
    hidden_out = pl.pallas_call(
        functools.partial(tail_kernel, bits, tp_count),
        out_shape=jax.ShapeDtypeStruct((rows, D), BF16),
        in_specs=[vmem] * 9,
        out_specs=vmem,
        scratch_shapes=[
            pltpu.VMEM((seq_count, GROUP * HD, TOK_DEV), BF16),
            pltpu.VMEM((seq_count, 8, TOK_DEV), F32),
            pltpu.VMEM((tp_count, rows, D), F32),
            pltpu.VMEM((tp_count, rows, D), BF16),
            pltpu.VMEM((tp_count - 1, rows, D), BF16),
            pltpu.VMEM((rows, D), BF16),
            *held,
            *held,
            *held,
            *[dma((seq_count,))] * 4,
            *[dma((tp_count - 1,))] * 2,
            *[dma((count, bits))] * 4,
        ],
        compiler_params=pltpu.CompilerParams(
            collective_id=1, has_side_effects=True, vmem_limit_bytes=52 << 20
        ),
        name="tail",
    )(
        acc,
        stat,
        buf,
        own_hidden,
        w_out,
        norm2_gain[None, :],
        w_gate[0],
        w_up[0],
        w_down[0],
    )
    return hidden_out, cache_out[:, :, None, :]


def solution(mesh):
    placed = (
        P("seq", None),
        P(),
        P(None, "tp"),
        P(None, "tp"),
        P(None, "tp"),
        P("tp", None),
        P(),
        P("seq", None, None),
        P("seq", None, None),
        P("seq", None, None),
        P("seq", None, "tp", None),
        P(),
        P(),
        P(("seq", "tp"), None),
        P(("seq", "tp"), None),
    )
    return jax.shard_map(
        on_device,
        mesh=mesh,
        in_specs=placed,
        out_specs=(P(("seq", "tp"), None), P("seq", None, "tp", None)),
        check_vma=False,
    )
```
